32 devices in a mesh: dp: 8 (over z, core), vocab: 4 (over y, x).
Axes of the slice: x: 2, y: 2, z: 4, core: 2. Of those that a mesh axis runs over, the one named last changes fastest.
Arguments:
- queries: bfloat16 [672, 8192], P('dp', 'vocab'), may hold values from -6 to 6
- residual: bfloat16 [672, 8192], P('dp', 'vocab'), may hold values from -16 to 16
- cache_k: bfloat16 [7, 32, 8, 512, 128], P(None, 'dp', 'vocab'), may hold values from -6 to 6, as said below
- cache_v: bfloat16 [7, 32, 8, 512, 128], P(None, 'dp', 'vocab'), may hold values from -6 to 6, as said below
- lengths: int32 [32, 7], P('dp'), may hold values from 128 to 512, as said below
- pairs: int32 [32, 21, 2], P('dp'), may hold values from 0 to 6, as said below
- out_weight: bfloat16 [8192, 8192], P('vocab'), may hold values from -1.5 to 1.5
- norm_gain: bfloat16 [8192], replicated, may hold values from 0.25 to 1.75
- head_weight: bfloat16 [8192, 8192], P(None, ('dp', 'vocab')), may hold values from -7 to 7
- answer_ids: int32 [2], replicated, may hold values from 0 to 8191
Outputs:
- verdict: float32 [672, 2], P('dp')
The draws below stay inside these ranges and needn't reach their ends.
Inputs may be any that keep to these rules, and one draw needn't show every extreme that they name: `lengths`: every response has at least 128 tokens, and in every prompt one response has exactly 512. `pairs`: for every prompt the 21 rows hold each unordered pair of two different responses once, as (first, second) in some order. `cache_k`: the slots of one key-value head hold equal copies. `cache_v`: the slots of one key-value head hold equal copies.
All inputs are finite; a program needn't handle non-finite values.
Results may differ from the reference program's by a relative error of at most 0.0011.
Values may be sent and summed in bfloat16 or wider, within the bound.
A program may use at most 192 MiB of HBM per device.

```python
import math
import jax
import jax.numpy as jnp
import numpy as np
from jax import lax

D = 8192
QH = 64
KVH = 8
HD = 128
RESP = 7
LMAX = 512
MIN_LEN = 128
PB = 4
GROUP = 8
HEAD_SLOTS = 8
NPAIR = 21
PROMPTS = 32
PAIRS = 672
VOCAB = 8192


def log_spread(key, array_shape, low_end, high_end):
    return jnp.exp(jax.random.uniform(key, array_shape, jnp.float32, math.log(low_end), math.log(high_end)))


def copy_slots(heads_array):
    return jnp.repeat(heads_array, HEAD_SLOTS // KVH, axis=2)


def draw_queries(key, part):
    array_shape = (PAIRS, QH * HD)
    factor = log_spread(jax.random.fold_in(key, 1), (PAIRS, 1), 0.3, 1.0)
    noise = jnp.clip(jax.random.normal(jax.random.fold_in(key, 2), array_shape, jnp.float32), -6.0, 6.0)
    return (noise * factor).astype(jnp.bfloat16)


def draw_cache_k(key, part):
    array_shape = (RESP, PROMPTS, KVH, LMAX, HD)
    factor = log_spread(jax.random.fold_in(key, 11), (RESP, PROMPTS, 1, LMAX, 1), 0.3, 1.0)
    noise = jnp.clip(jax.random.normal(jax.random.fold_in(key, 12), array_shape, jnp.float32), -6.0, 6.0)
    return copy_slots(noise * factor).astype(jnp.bfloat16)


def draw_cache_v(key, part):
    array_shape = (RESP, PROMPTS, KVH, LMAX, HD)
    return copy_slots(jnp.clip(jax.random.normal(jax.random.fold_in(key, 61), array_shape, jnp.float32), -6.0, 6.0)).astype(jnp.bfloat16)


def draw_residual(key, part):
    array_shape = (PAIRS, D)
    row_scale = log_spread(jax.random.fold_in(key, 21), (PAIRS, 1), 0.5, 1.6)
    column_scale = log_spread(jax.random.fold_in(key, 22), (1, D), 0.5, 1.6)
    noise = jnp.clip(jax.random.normal(jax.random.fold_in(key, 23), array_shape, jnp.float32), -6.0, 6.0)
    return (noise * row_scale * column_scale).astype(jnp.bfloat16)


def draw_head_weight(key, part):
    array_shape = (D, VOCAB)
    column = lax.broadcasted_iota(jnp.int32, (1, VOCAB), 1)
    column_norm = 2.5 + 0.5 * column.astype(jnp.float32) / VOCAB
    factor = column_norm / math.sqrt(D)
    noise = jnp.clip(jax.random.normal(jax.random.fold_in(key, 32), array_shape, jnp.float32), -6.0, 6.0)
    return (noise * factor).astype(jnp.bfloat16)


def draw_lengths(key, part):
    drawn_lengths = jax.random.randint(jax.random.fold_in(key, 41), (PROMPTS, RESP), MIN_LEN, LMAX + 1)
    longest = jax.random.randint(jax.random.fold_in(key, 42), (PROMPTS, 1), 0, RESP)
    slot_index = lax.broadcasted_iota(jnp.int32, (PROMPTS, RESP), 1)
    return jnp.where(slot_index == longest, LMAX, drawn_lengths).astype(jnp.int32)


def draw_pairs(key, part):
    lower_np, upper_np = np.triu_indices(RESP, 1)
    lower_ids = jnp.asarray(lower_np, jnp.int32)
    upper_ids = jnp.asarray(upper_np, jnp.int32)
    orders = jax.vmap(lambda sub_key: jax.random.permutation(sub_key, NPAIR))(jax.random.split(jax.random.fold_in(key, 51), PROMPTS))
    flip_bits = jax.random.randint(jax.random.fold_in(key, 52), (PROMPTS, NPAIR), 0, 2)
    low_ids = jnp.take(lower_ids, orders)
    high_ids = jnp.take(upper_ids, orders)
    leading_ids = jnp.where(flip_bits == 1, high_ids, low_ids)
    second_ids = jnp.where(flip_bits == 1, low_ids, high_ids)
    return jnp.stack([leading_ids, second_ids], axis=-1).astype(jnp.int32)


def levels(own_key, shape, cuts, smallest, high):
    def one(axis_at, blocks):
        heights = jax.random.uniform(jax.random.fold_in(jax.random.fold_in(own_key, 6), axis_at), (blocks,), jnp.float32, smallest / len(cuts), high / len(cuts))
        return jnp.repeat(jnp.exp(heights), shape[axis_at] // blocks).reshape((-1,) + (1,) * (len(shape) - axis_at - 1))

    gain = one(*cuts[0])
    for cut in cuts[1:]:
        gain = gain * one(*cut)
    return gain


def gaussian(rng, extent, deviation, limit, cuts=(), kind=jnp.bfloat16):
    drawn = deviation * jax.random.normal(rng, extent, jnp.float32)
    if cuts:
        drawn = drawn * levels(rng, extent, cuts, -0.22, 0.18)
    return jnp.clip(drawn, -limit, limit).astype(kind)


def setup_inputs(seed: int = 0) -> dict:
    splits = jax.random.split(jax.random.key(seed), 11)
    return {
        "queries": draw_queries(jax.random.fold_in(splits[10], 71), 0),
        "residual": draw_residual(jax.random.fold_in(splits[10], 71), 0),
        "cache_k": draw_cache_k(jax.random.fold_in(splits[10], 71), 0),
        "cache_v": draw_cache_v(jax.random.fold_in(splits[10], 71), 0),
        "lengths": draw_lengths(jax.random.fold_in(splits[10], 71), 0),
        "pairs": draw_pairs(jax.random.fold_in(splits[10], 71), 0),
        "out_weight": gaussian(splits[6], (QH * HD, D), (QH * HD // LMAX) ** -0.5, 1.5, ((0, 4),)),
        "norm_gain": jnp.clip(1.0 + 0.15 * jax.random.normal(splits[7], (D,), jnp.float32), 0.25, 1.75).astype(jnp.bfloat16),
        "head_weight": draw_head_weight(jax.random.fold_in(splits[10], 71), 0),
        "answer_ids": jax.random.randint(splits[9], (2,), 0, VOCAB).astype(jnp.int32),
    }


def prompt_verdicts(prompt, queries, residual, cache_k, cache_v, lengths, pairs, out_weight, norm_gain, head_weight, answer_ids):
    answers = jnp.arange(RESP, dtype=jnp.int32)
    slot_index = ((prompt + answers * PB) % PROMPTS).astype(jnp.int32)
    stride = HEAD_SLOTS // KVH
    keys_all = cache_k[answers, slot_index][:, ::stride]
    values_all = cache_v[answers, slot_index][:, ::stride]
    listed = pairs[prompt]
    leading = listed[:, 0]
    second = listed[:, 1]
    key_rows = jnp.concatenate([keys_all[leading], keys_all[second]], axis=2)
    value_rows = jnp.concatenate([values_all[leading], values_all[second]], axis=2)
    spans = lengths[prompt]
    position = jnp.arange(LMAX, dtype=jnp.int32)[None, :]
    usable = jnp.concatenate([position < spans[leading][:, None], position < spans[second][:, None]], axis=1)
    row_start = (prompt * NPAIR).astype(jnp.int32)
    query_rows = lax.dynamic_slice_in_dim(queries, row_start, NPAIR, 0).reshape(NPAIR, KVH, GROUP, HD)
    scores = jnp.einsum('nagh,nalh->nagl', query_rows.astype(jnp.float32), key_rows.astype(jnp.float32)) / math.sqrt(HD)
    scores = jnp.where(usable[:, None, None, :], scores, -jnp.inf)
    highest = lax.optimization_barrier(jnp.max(scores, axis=-1, keepdims=True))
    exponent = jnp.exp(scores - highest)
    weights = (exponent / lax.optimization_barrier(jnp.sum(exponent, axis=-1, keepdims=True))).astype(jnp.bfloat16)
    attended = jnp.einsum('nagl,nalh->nagh', weights.astype(jnp.float32), value_rows.astype(jnp.float32))
    attended = attended.astype(jnp.bfloat16).reshape(NPAIR, QH * HD)
    residual_rows = lax.dynamic_slice_in_dim(residual, row_start, NPAIR, 0)
    hidden = (jnp.dot(attended, out_weight, preferred_element_type=jnp.float32) + residual_rows.astype(jnp.float32)).astype(jnp.bfloat16)
    widened = hidden.astype(jnp.float32)
    factor = lax.rsqrt(lax.optimization_barrier(jnp.mean(widened * widened, axis=-1, keepdims=True)) + 1e-05)
    normed = (widened * factor * norm_gain.astype(jnp.float32)).astype(jnp.bfloat16)
    logits = jnp.dot(normed, head_weight, preferred_element_type=jnp.float32)
    top_logit = lax.optimization_barrier(jnp.max(logits, axis=-1))
    log_total = top_logit + jnp.log(lax.optimization_barrier(jnp.sum(jnp.exp(logits - top_logit[:, None]), axis=-1)))
    return jnp.stack([logits[:, answer_ids[0]] - log_total, logits[:, answer_ids[1]] - log_total], axis=-1)

def reference(queries, residual, cache_k, cache_v, lengths, pairs, out_weight, norm_gain, head_weight, answer_ids):

    def one_prompt(prompt):
        return prompt_verdicts(prompt, queries, residual, cache_k, cache_v, lengths, pairs, out_weight, norm_gain, head_weight, answer_ids)
    verdict = lax.map(one_prompt, jnp.arange(PROMPTS, dtype=jnp.int32))
    return verdict.reshape(PAIRS, 2)
```

```python
import functools
import math

import jax
import jax.numpy as jnp
from jax import lax
from jax.experimental import pallas as pl
from jax.experimental.pallas import tpu as pltpu
from jax.sharding import PartitionSpec as P

MESH = pl.DeviceIdType.MESH
F32 = jnp.float32
BF16 = jnp.bfloat16


def up(n, m):
    return -(-n // m) * m


def remote(src, dst, send, recv, device):
    return pltpu.make_async_remote_copy(
        src_ref=src, dst_ref=dst, send_sem=send, recv_sem=recv,
        device_id=device, device_id_type=MESH,
    )


def greet(partners):
    barrier = pltpu.get_barrier_semaphore()
    for device in partners:
        pl.semaphore_signal(barrier, inc=1, device_id=device, device_id_type=MESH)
    pl.semaphore_wait(barrier, len(partners))


def attend_kernel(
    n, pick_ref, place_ref, q_ref, lens_ref, k_hbm, v_hbm, out_ref,
    k_ref, v_ref, qs, qr, lr, ob, orecv, st, strecv,
    kv_sem, q_send, q_recv, l_send, l_recv, o_send, o_recv, s_send, s_recv,
):
    answers, prompts, heads, longest, hd = k_hbm.shape
    span = qr.shape[3]
    me, col = lax.axis_index("dp"), lax.axis_index("vocab")
    loads = []
    for i in range(answers):
        for which, (src, dst) in enumerate(((k_hbm, k_ref), (v_hbm, v_ref))):
            load = pltpu.make_async_copy(src.at[i], dst.at[i], kv_sem.at[which, i])
            load.start()
            loads.append(load)
    shifts = sorted({s % n for i in range(1, answers) for s in (i, -i)})
    for p in range(prompts):
        for c in range(heads):
            qs[p, c] = jnp.dot(
                pick_ref[p], q_ref[p, c], preferred_element_type=F32
            ).astype(BF16)
    greet([(lax.rem(me + s, n), col) for s in shifts])
    order = [1, 2, 6, 3, 5, 4] if answers == 7 else list(range(1, answers))
    q_out, l_out, o_out, s_out = {}, {}, {}, {}
    for i in order:
        ahead = (lax.rem(me + i, n), col)
        behind = (lax.rem(me + n - i, n), col)
        rows = pl.ds(i * span, span)
        q_out[i] = remote(
            qs.at[:, :, rows], qr.at[i], q_send.at[i], q_recv.at[i], ahead)
        l_out[i] = remote(lens_ref.at[i], lr.at[i], l_send.at[i], l_recv.at[i], ahead)
        o_out[i] = remote(
            ob.at[i], orecv.at[:, :, rows], o_send.at[i], o_recv.at[i], behind)
        s_out[i] = remote(
            st.at[i], strecv.at[rows], s_send.at[i], s_recv.at[i], behind)
        q_out[i].start()
        l_out[i].start()
    scale = 1.0 / math.sqrt(hd)
    for i in [0] + order:
        loads[2 * i].wait()
        loads[2 * i + 1].wait()
        if i:
            q_out[i].wait_recv()
            l_out[i].wait_recv()
        lane = lax.broadcasted_iota(jnp.int32, (span, 128), 1)
        position = lax.broadcasted_iota(jnp.int32, (span, longest), 1)
        stats = jnp.zeros((span, 128), F32)
        for p in range(prompts):
            limit = (lr[i, p : p + 1, 0:1] if i else lens_ref[0, p : p + 1, 0:1])
            for c in range(heads):
                q = qr[i, p, c] if i else qs[p, c, 0:span]
                s = lax.dot_general(
                    q, k_ref[i, p, c], (((1,), (1,)), ((), ())),
                    preferred_element_type=F32,
                ) * scale
                s = jnp.where(position < limit, s, -jnp.inf)
                top = jnp.max(s, axis=1, keepdims=True)
                e = jnp.exp(s - top)
                total = jnp.sum(e, axis=1, keepdims=True)
                o = jnp.dot(e.astype(BF16), v_ref[i, p, c], preferred_element_type=F32)
                o = (o / total).astype(BF16)
                if i:
                    ob[i, p, c] = o
                else:
                    orecv[p, c, 0:span] = o
                lse = top + jnp.log(total)
                high = lse.astype(BF16).astype(F32)
                mid = (lse - high).astype(BF16).astype(F32)
                low = lse - high - mid
                at = 3 * (p * heads + c)
                stats = jnp.where(lane == at, high, stats)
                stats = jnp.where(lane == at + 1, mid, stats)
                stats = jnp.where(lane == at + 2, low, stats)
        if i:
            st[i] = stats.astype(BF16)
            o_out[i].start()
            s_out[i].start()
        else:
            strecv[0:span] = stats.astype(BF16)
    for i in order:
        o_out[i].wait_recv()
        s_out[i].wait_recv()
    half = out_ref.shape[2]
    for p in range(prompts):
        place = place_ref[p]
        both = jnp.dot(place, strecv[...], preferred_element_type=F32)
        for c in range(heads):
            at = 3 * (p * heads + c)
            lse = both[:, at : at + 1] + both[:, at + 1 : at + 2] + both[:, at + 2 : at + 3]
            first, second = lse[:half], lse[half:]
            top = jnp.maximum(first, second)
            first, second = jnp.exp(first - top), jnp.exp(second - top)
            o = jnp.dot(place, orecv[p, c], preferred_element_type=F32)
            mixed = (first * o[:half] + second * o[half:]) / (first + second)
            out_ref[p, c] = mixed.astype(BF16)
    for i in order:
        for copy in (q_out[i], l_out[i], o_out[i], s_out[i]):
            copy.wait_send()


def tail_kernel(
    nd, nv, width, part_ref, res_ref, gain_ref, w_ref, ids_ref, out_ref,
    sb, rb, hid, sq, sqr, g, stat, statr, vrow,
    p_send, p_recv, q_send, q_recv, g_send, g_recv, t_send, t_recv, v_send, v_recv,
):
    rows, share = res_ref.shape
    me, col = lax.axis_index("dp"), lax.axis_index("vocab")
    vpeer = {j: lax.rem(col + j, nv) for j in range(1, nv)}
    dpeer = {j: lax.rem(me + j, nd) for j in range(1, nd)}
    greet([(me, vpeer[j]) for j in vpeer] + [(dpeer[j], col) for j in dpeer])

    def columns(v):
        return pl.ds(pl.multiple_of(v * share, 128), share)

    parts = {}
    for j in vpeer:
        sb[j] = part_ref[:, columns(vpeer[j])].astype(BF16)
        parts[j] = remote(
            sb.at[j], rb.at[j], p_send.at[j], p_recv.at[j], (me, vpeer[j]))
        parts[j].start()
    for j in vpeer:
        parts[j].wait_recv()
    step = 256 if share % 256 == 0 else 128
    squares = jnp.zeros((rows, 128), F32)
    for t in range(0, share, step):
        total = part_ref[:, pl.ds(pl.multiple_of(col * share + t, 128), step)]
        total = total + res_ref[:, t : t + step].astype(F32)
        for j in vpeer:
            total = total + rb[j, :, t : t + step].astype(F32)
        total = total.astype(BF16)
        hid[:, t : t + step] = total
        total = total.astype(F32)
        for u in range(0, step, 128):
            squares = squares + total[:, u : u + 128] * total[:, u : u + 128]
    sq[...] = squares
    exch = {}
    for j in vpeer:
        exch[j] = remote(
            sq, sqr.at[j], q_send.at[j], q_recv.at[j], (me, vpeer[j]))
        exch[j].start()
    for j in vpeer:
        exch[j].wait_recv()
        squares = squares + sqr[j]
    mean = jnp.sum(squares, axis=1, keepdims=True) * (1.0 / (share * nv))
    factor = lax.rsqrt(mean + 1e-05)
    for t in range(0, share, step):
        block = hid[:, t : t + step].astype(F32) * factor
        g[me, col, :, t : t + step] = (
            block * gain_ref[0:1, t : t + step].astype(F32)
        ).astype(BF16)

    core = lax.rem(me, 2)
    sib = me + 1 - 2 * core
    sent = []

    def push(e, v, device, slot):
        block = g.at[e, v]
        copy = remote(block, block, g_send.at[slot], g_recv.at[e, v], device)
        copy.start()
        sent.append(copy)

    def arrived(e, v):
        block = g.at[e, v]
        remote(block, block, g_send.at[0], g_recv.at[e, v], (sib, col)).wait_recv()

    nz = nd // 2
    lines = [lax.rem(me + 2 * s, nd) for s in range(nz)]
    slot = 0
    for s in range(1, nz):
        push(me, col, (lines[s], col), slot)
        slot += 1
    for j in vpeer:
        push(me, col, (me, vpeer[j]), slot)
        slot += 1
    push(me, col, (sib, col), slot)
    slot += 1
    for s in range(1, nz):
        arrived(lines[s], col)
        for j in vpeer:
            push(lines[s], col, (me, vpeer[j]), slot)
            slot += 1
        push(lines[s], col, (sib, col), slot)
        slot += 1

    base = (me * nv + col) * width
    cols = lax.broadcasted_iota(jnp.int32, (rows, width), 1) + base
    lane = lax.broadcasted_iota(jnp.int32, (rows, 128), 1)
    tail = jnp.zeros((128 - rows % 128, 128), F32) if rows % 128 else None

    def head(e):
        def body(v, acc):
            return acc + jnp.dot(g[e, v], w_ref[v], preferred_element_type=F32)

        logits = lax.fori_loop(0, nv, body, jnp.zeros((rows, width), F32))
        top = jnp.max(logits, axis=1, keepdims=True)
        total = jnp.sum(jnp.exp(logits - top), axis=1, keepdims=True)
        yes = jnp.sum(jnp.where(cols == ids_ref[0:1, 0:1], logits, 0.0), axis=1, keepdims=True)
        no = jnp.sum(jnp.where(cols == ids_ref[1:2, 0:1], logits, 0.0), axis=1, keepdims=True)
        tile = jnp.where(lane == 0, top, 0.0)
        for at, what in ((1, total), (2, yes), (3, no)):
            tile = jnp.where(lane == at, what, tile)
        if tail is not None:
            tile = jnp.concatenate([tile, tail], axis=0)
        stat[e] = jnp.transpose(tile)[0:8]

    for s in range(nz):
        for j in vpeer:
            arrived(lines[s], vpeer[j])
            push(lines[s], vpeer[j], (sib, col), slot)
            slot += 1
    stats = []

    def deliver(e, at):
        copy = remote(
            stat.at[e], statr.at[me], t_send.at[at], t_recv.at[me], (e, col))
        copy.start()
        stats.append(copy)

    for s in range(nz):
        head(lines[s])
        if s:
            deliver(lines[s], 2 * s)
    for s in range(nz):
        other = lax.rem(sib + 2 * s, nd)
        for v in range(nv):
            arrived(other, v)
        head(other)
        deliver(other, 2 * s + 1)
    statr[me] = stat[me]
    for j in dpeer:
        e = dpeer[j]
        remote(
            stat.at[e], statr.at[e], t_send.at[0], t_recv.at[e], (e, col)
        ).wait_recv()

    def merge(ref, count):
        top = ref[0, 0:1]
        for e in range(1, count):
            top = jnp.maximum(top, ref[e, 0:1])
        total = jnp.zeros_like(top)
        yes = jnp.zeros_like(top)
        no = jnp.zeros_like(top)
        for e in range(count):
            total = total + ref[e, 1:2] * jnp.exp(ref[e, 0:1] - top)
            yes = yes + ref[e, 2:3]
            no = no + ref[e, 3:4]
        return top, total, yes, no

    top, total, yes, no = merge(statr, nd)
    vrow[col] = jnp.concatenate(
        [top, total, yes, no, jnp.zeros((4, top.shape[1]), F32)], axis=0)
    last = {}
    for j in vpeer:
        last[j] = remote(
            vrow.at[col], vrow.at[col], v_send.at[j], v_recv.at[col], (me, vpeer[j]))
        last[j].start()
    for j in vpeer:
        v = vpeer[j]
        remote(
            vrow.at[v], vrow.at[v], v_send.at[0], v_recv.at[v], (me, v)
        ).wait_recv()
    top, total, yes, no = merge(vrow, nv)
    log_total = top + jnp.log(total)
    out_ref[...] = jnp.concatenate(
        [yes - log_total, no - log_total, jnp.zeros((6, top.shape[1]), F32)], axis=0)
    for copy in [*parts.values(), *exch.values(), *sent, *stats, *last.values()]:
        copy.wait_send()


def dma(*shape):
    return pltpu.SemaphoreType.DMA(shape)


def selectors(pairs, answers, group, span, slots):
    prompts, per_prompt, _ = pairs.shape
    ids = jnp.arange(answers, dtype=jnp.int32)
    chosen = pairs[:, None, :, :] == ids[None, :, None, None]
    involved = chosen[..., 0] | chosen[..., 1]
    k = jnp.arange(per_prompt, dtype=jnp.int32)
    rank = jnp.sum(
        (involved[:, :, None, :] & (k[None, :] < k[:, None])[None, None]).astype(jnp.int32), -1)
    key = pairs * span + jnp.sum(
        jnp.where(chosen, rank[..., None], 0), axis=1) * group
    wide = jnp.repeat(key, group, axis=1) + jnp.tile(
        jnp.arange(group, dtype=jnp.int32), per_prompt)[None, :, None]
    wide = jnp.pad(wide, ((0, 0), (0, slots - wide.shape[1]), (0, 0)), constant_values=-1)
    row = jnp.arange(answers * span, dtype=jnp.int32)
    first, second = wide[:, :, 0], wide[:, :, 1]
    pick = (row[None, :, None] == first[:, None, :]) | (row[None, :, None] == second[:, None, :])
    both = jnp.concatenate([first, second], axis=1)
    place = both[:, :, None] == row[None, None, :]
    return pick.astype(BF16), place.astype(BF16)


def local(
    queries, residual, cache_k, cache_v, lengths, pairs, out_weight, norm_gain,
    head_weight, answer_ids,
):
    nd, nv = lax.axis_size("dp"), lax.axis_size("vocab")
    answers, prompts, heads, longest, hd = cache_k.shape
    pair_rows = queries.shape[0]
    per_prompt = pairs.shape[1]
    group = queries.shape[1] // hd // heads
    span = up((answers - 1) * group, 16)
    slots = up(per_prompt * group, 16)
    pick, place = selectors(pairs, answers, group, span, slots)
    q = queries.reshape(prompts, per_prompt, heads, group, hd).transpose(0, 2, 1, 3, 4)
    q = q.reshape(prompts, heads, per_prompt * group, hd)
    q = jnp.pad(q, ((0, 0), (0, 0), (0, slots - per_prompt * group), (0, 0)))
    lens = jnp.pad(lengths.T, ((0, 0), (0, up(prompts, 8) - prompts)))
    lens = jnp.broadcast_to(lens[:, :, None], lens.shape + (128,))
    vm = pl.BlockSpec(memory_space=pltpu.VMEM)
    hbm = pl.BlockSpec(memory_space=pl.ANY)
    attended = pl.pallas_call(
        functools.partial(attend_kernel, nd),
        out_shape=jax.ShapeDtypeStruct((prompts, heads, slots, hd), BF16),
        in_specs=[vm, vm, vm, vm, hbm, hbm],
        out_specs=vm,
        scratch_shapes=[
            pltpu.VMEM(cache_k.shape, BF16),
            pltpu.VMEM(cache_k.shape, BF16),
            pltpu.VMEM((prompts, heads, answers * span, hd), BF16),
            pltpu.VMEM((answers, prompts, heads, span, hd), BF16),
            pltpu.VMEM(lens.shape, jnp.int32),
            pltpu.VMEM((answers, prompts, heads, span, hd), BF16),
            pltpu.VMEM((prompts, heads, answers * span, hd), BF16),
            pltpu.VMEM((answers, span, 128), BF16),
            pltpu.VMEM((answers * span, 128), BF16),
            dma(2, answers),
        ] + [dma(answers)] * 8,
        compiler_params=pltpu.CompilerParams(
            collective_id=0, has_side_effects=True, vmem_limit_bytes=40 << 20),
    )(pick, place, q, lens, cache_k, cache_v)
    attended = attended[:, :, : per_prompt * group].reshape(
        prompts, heads, per_prompt, group, hd).transpose(0, 2, 1, 3, 4)
    rows = up(pair_rows, 16)
    attended = jnp.pad(
        attended.reshape(pair_rows, heads * group * hd), ((0, rows - pair_rows), (0, 0)))
    partial = jnp.dot(attended, out_weight, preferred_element_type=F32)
    share = residual.shape[1]
    width = head_weight.shape[1]
    res = jnp.pad(residual, ((0, rows - pair_rows), (0, 0)))
    own_gain = lax.dynamic_slice_in_dim(norm_gain, lax.axis_index("vocab") * share, share, 0)
    own_gain = jnp.broadcast_to(own_gain.astype(F32)[None], (8, share))
    ids = jnp.broadcast_to(jnp.pad(answer_ids, (0, 6))[:, None], (8, 128))
    wide = up(rows, 128)
    verdict = pl.pallas_call(
        functools.partial(tail_kernel, nd, nv, width),
        out_shape=jax.ShapeDtypeStruct((8, wide), F32),
        in_specs=[vm] * 5,
        out_specs=vm,
        scratch_shapes=[
            pltpu.VMEM((nv, rows, share), BF16),
            pltpu.VMEM((nv, rows, share), BF16),
            pltpu.VMEM((rows, share), BF16),
            pltpu.VMEM((rows, 128), F32),
            pltpu.VMEM((nv, rows, 128), F32),
            pltpu.VMEM((nd, nv, rows, share), BF16),
            pltpu.VMEM((nd, 8, wide), F32),
            pltpu.VMEM((nd, 8, wide), F32),
            pltpu.VMEM((nv, 8, wide), F32),
            dma(nv), dma(nv), dma(nv), dma(nv),
            dma((nd // 2) * (2 * nv + 1)), dma(nd, nv),
            dma(nd), dma(nd), dma(nv), dma(nv),
        ],
        compiler_params=pltpu.CompilerParams(
            collective_id=1, has_side_effects=True, vmem_limit_bytes=52 << 20),
    )(partial, res, own_gain, head_weight.reshape(nv, share, width), ids)
    return verdict[:2, :pair_rows].T


def solution(mesh):
    in_specs = (
        P("dp", "vocab"),
        P("dp", "vocab"),
        P(None, "dp", "vocab", None, None),
        P(None, "dp", "vocab", None, None),
        P("dp", None),
        P("dp", None, None),
        P("vocab", None),
        P(),
        P(None, ("dp", "vocab")),
        P(),
    )
    out_specs = P("dp", None)
    return jax.shard_map(local, mesh=mesh, in_specs=in_specs, out_specs=out_specs, check_vma=False)
```

```python
import functools
import math

import jax
import jax.numpy as jnp
from jax import lax
from jax.experimental import pallas as pl
from jax.experimental.pallas import tpu as pltpu
from jax.sharding import PartitionSpec as P

MESH = pl.DeviceIdType.MESH
F32 = jnp.float32
BF16 = jnp.bfloat16
BUFS = 4


def up(n, m):
    return -(-n // m) * m


def remote(src, dst, send, recv, device):
    return pltpu.make_async_remote_copy(
        src_ref=src, dst_ref=dst, send_sem=send, recv_sem=recv,
        device_id=device, device_id_type=MESH,
    )


def greet(partners):
    barrier = pltpu.get_barrier_semaphore()
    for device in partners:
        pl.semaphore_signal(barrier, inc=1, device_id=device, device_id_type=MESH)
    pl.semaphore_wait(barrier, len(partners))


def attend_kernel(
    n, pick_ref, place_ref, q_ref, lens_ref, k_hbm, v_hbm, out_ref,
    k_ref, v_ref, qs, qr, lr, ob, orecv, st, strecv,
    kv_sem, q_send, q_recv, l_send, l_recv, o_send, o_recv, s_send, s_recv,
):
    answers, prompts, heads, longest, hd = k_hbm.shape
    span = qr.shape[3]
    me, col = lax.axis_index("dp"), lax.axis_index("vocab")
    loads = []
    for i in range(answers):
        for which, (src, dst) in enumerate(((k_hbm, k_ref), (v_hbm, v_ref))):
            load = pltpu.make_async_copy(src.at[i], dst.at[i], kv_sem.at[which, i])
            load.start()
            loads.append(load)
    shifts = sorted({s % n for i in range(1, answers) for s in (i, -i)})
    for p in range(prompts):
        for c in range(heads):
            qs[p, c] = jnp.dot(
                pick_ref[p], q_ref[p, c], preferred_element_type=F32
            ).astype(BF16)
    greet([(lax.rem(me + s, n), col) for s in shifts])
    order = [1, 2, 6, 3, 5, 4] if answers == 7 else list(range(1, answers))
    q_out, l_out, o_out, s_out = {}, {}, {}, {}
    for i in order:
        ahead = (lax.rem(me + i, n), col)
        behind = (lax.rem(me + n - i, n), col)
        rows = pl.ds(i * span, span)
        q_out[i] = remote(
            qs.at[:, :, rows], qr.at[i], q_send.at[i], q_recv.at[i], ahead)
        l_out[i] = remote(lens_ref.at[i], lr.at[i], l_send.at[i], l_recv.at[i], ahead)
        o_out[i] = remote(
            ob.at[i], orecv.at[:, :, rows], o_send.at[i], o_recv.at[i], behind)
        s_out[i] = remote(
            st.at[i], strecv.at[rows], s_send.at[i], s_recv.at[i], behind)
        q_out[i].start()
        l_out[i].start()
    scale = 1.0 / math.sqrt(hd)
    for i in [0] + order:
        loads[2 * i].wait()
        loads[2 * i + 1].wait()
        if i:
            q_out[i].wait_recv()
            l_out[i].wait_recv()
        lane = lax.broadcasted_iota(jnp.int32, (span, 128), 1)
        position = lax.broadcasted_iota(jnp.int32, (span, longest), 1)
        stats = jnp.zeros((span, 128), F32)
        for p in range(prompts):
            limit = (lr[i, p : p + 1, 0:1] if i else lens_ref[0, p : p + 1, 0:1])
            for c in range(heads):
                q = qr[i, p, c] if i else qs[p, c, 0:span]
                s = lax.dot_general(
                    q, k_ref[i, p, c], (((1,), (1,)), ((), ())),
                    preferred_element_type=F32,
                ) * scale
                s = jnp.where(position < limit, s, -jnp.inf)
                top = jnp.max(s, axis=1, keepdims=True)
                e = jnp.exp(s - top)
                total = jnp.sum(e, axis=1, keepdims=True)
                big = e.astype(BF16)
                small = (e - big.astype(F32)).astype(BF16)
                o = jnp.dot(big, v_ref[i, p, c], preferred_element_type=F32)
                o = o + jnp.dot(small, v_ref[i, p, c], preferred_element_type=F32)
                o = (o / total).astype(BF16)
                if i:
                    ob[i, p, c] = o
                else:
                    orecv[p, c, 0:span] = o
                lse = top + jnp.log(total)
                high = lse.astype(BF16).astype(F32)
                mid = (lse - high).astype(BF16).astype(F32)
                low = lse - high - mid
                at = 3 * (p * heads + c)
                stats = jnp.where(lane == at, high, stats)
                stats = jnp.where(lane == at + 1, mid, stats)
                stats = jnp.where(lane == at + 2, low, stats)
        if i:
            st[i] = stats.astype(BF16)
            o_out[i].start()
            s_out[i].start()
        else:
            strecv[0:span] = stats.astype(BF16)
    for i in order:
        o_out[i].wait_recv()
        s_out[i].wait_recv()
    half = place_ref.shape[1] // 2
    group = out_ref.shape[1] // heads // hd
    each = half // group
    for p in range(prompts):
        place = place_ref[p]
        both = jnp.dot(place, strecv[...], preferred_element_type=F32)
        for c in range(heads):
            at = 3 * (p * heads + c)
            lse = both[:, at : at + 1] + both[:, at + 1 : at + 2] + both[:, at + 2 : at + 3]
            first, second = lse[:half], lse[half:]
            top = jnp.maximum(first, second)
            first, second = jnp.exp(first - top), jnp.exp(second - top)
            o = jnp.dot(place, orecv[p, c], preferred_element_type=F32)
            mixed = (first * o[:half] + second * o[half:]) / (first + second)
            mixed = mixed.astype(BF16)
            for j in range(group):
                at = (c * group + j) * hd
                out_ref[p * each : (p + 1) * each, at : at + hd] = (
                    mixed[j * each : (j + 1) * each])
    for i in order:
        for copy in (q_out[i], l_out[i], o_out[i], s_out[i]):
            copy.wait_send()


def tail_kernel(
    nd, nv, width, chunk, att_ref, ow_hbm, res_ref, gain_ref, w_ref, ids_ref, out_ref,
    wb, own, sb, rb, hid, sq, sqr, g, stat, statr, vrow,
    w_sem, p_send, p_recv, q_send, q_recv, g_send, g_recv, t_send, t_recv, v_send, v_recv,
):
    rows, share = res_ref.shape
    me, col = lax.axis_index("dp"), lax.axis_index("vocab")
    square = nv == 4
    if square:
        vpeer = {
            3: 3 - col, 1: col + 1 - 2 * lax.rem(col, 2), 2: lax.rem(col + 2, nv)}
    else:
        vpeer = {j: lax.rem(col + j, nv) for j in range(1, nv)}
    dpeer = {j: lax.rem(me + j, nd) for j in range(1, nd)}
    per = share // chunk
    todo = [(j, t) for j in [*vpeer, 0] for t in range(per)]

    def load(at):
        j, t = todo[at]
        v = vpeer[j] if j else col
        start = pl.multiple_of(v * share + t * chunk, 128)
        return pltpu.make_async_copy(
            ow_hbm.at[:, pl.ds(start, chunk)], wb.at[at % BUFS], w_sem.at[at % BUFS])

    for at in range(min(BUFS, len(todo))):
        load(at).start()
    greet([(me, vpeer[j]) for j in vpeer] + [(dpeer[j], col) for j in dpeer])
    step = 256 if chunk % 256 == 0 else 128
    parts = {}
    for at, (j, t) in enumerate(todo):
        load(at).wait()

        def tile(u, carry, at=at, j=j, t=t):
            here = pl.ds(pl.multiple_of(u * step, step), step)
            there = pl.ds(pl.multiple_of(t * chunk + u * step, step), step)
            got = jnp.dot(
                att_ref[...], wb[at % BUFS, :, here], preferred_element_type=F32)
            if j:
                sb[j, :, there] = got.astype(BF16)
            else:
                own[:, there] = got + res_ref[:, there].astype(F32)
            return carry

        lax.fori_loop(0, chunk // step, tile, 0)
        if at + BUFS < len(todo):
            load(at + BUFS).start()
        if j:
            there = pl.ds(t * chunk, chunk)
            parts[j, t] = remote(
                sb.at[j, :, there], rb.at[j, :, there],
                p_send.at[j, t], p_recv.at[j, t], (me, vpeer[j]))
            parts[j, t].start()
    squares = jnp.zeros((rows, 128), F32)
    for t in range(0, share, step):
        if t % chunk == 0:
            for j in vpeer:
                parts[j, t // chunk].wait_recv()
        total = own[:, t : t + step]
        for j in vpeer:
            total = total + rb[j, :, t : t + step].astype(F32)
        total = total.astype(BF16)
        hid[:, t : t + step] = total
        total = total.astype(F32)
        for u in range(0, step, 128):
            squares = squares + total[:, u : u + 128] * total[:, u : u + 128]
    sq[...] = squares
    exch = {}
    for j in vpeer:
        exch[j] = remote(
            sq, sqr.at[j], q_send.at[j], q_recv.at[j], (me, vpeer[j]))
        exch[j].start()
    for j in vpeer:
        exch[j].wait_recv()
        squares = squares + sqr[j]
    mean = jnp.sum(squares, axis=1, keepdims=True) * (1.0 / (share * nv))
    factor = lax.rsqrt(mean + 1e-05)
    for t in range(0, share, step):
        block = hid[:, t : t + step].astype(F32) * factor
        g[me, col, :, t : t + step] = (
            block * gain_ref[0:1, t : t + step].astype(F32)
        ).astype(BF16)

    core = lax.rem(me, 2)
    sib = me + 1 - 2 * core
    sent = []

    def push(e, v, device, slot):
        block = g.at[e, v]
        copy = remote(block, block, g_send.at[slot], g_recv.at[e, v], device)
        copy.start()
        sent.append(copy)

    def arrived(e, v):
        block = g.at[e, v]
        remote(block, block, g_send.at[0], g_recv.at[e, v], (sib, col)).wait_recv()

    nz = nd // 2
    z = lax.div(me, 2)
    upper = lax.div(z, nz // 2)
    mirrored = z + upper * (nz - 1 - 2 * z)
    lines = [me]
    for t in range(nz - 1):
        at = t + lax.div(t - mirrored + nz, nz)
        lines.append(2 * (at + upper * (nz - 1 - 2 * at)) + core)
    slot = [0]

    def send(e, v, device):
        push(e, v, device, slot[0])
        slot[0] += 1

    direct = [1, 2] if square else list(vpeer)

    def spread(s):
        e = lines[s]
        if s:
            arrived(e, col)
        for j in direct:
            send(e, col, (me, vpeer[j]))
        if s == 0:
            for t in reversed(range(1, nz)):
                send(e, col, (lines[t], col))
        send(e, col, (sib, col))

    def collect(s):
        e = lines[s]
        for j in direct:
            arrived(e, vpeer[j])
            if square and j == 1 + s % 2:
                send(e, vpeer[j], (me, vpeer[3 - j]))
            send(e, vpeer[j], (sib, col))
        if square:
            arrived(e, vpeer[3])
            send(e, vpeer[3], (sib, col))

    base = (me * nv + col) * width
    cols = lax.broadcasted_iota(jnp.int32, (rows, width), 1) + base
    lane = lax.broadcasted_iota(jnp.int32, (rows, 128), 1)
    tail = jnp.zeros((128 - rows % 128, 128), F32) if rows % 128 else None

    def head(e):
        def body(v, acc):
            return acc + jnp.dot(g[e, v], w_ref[v], preferred_element_type=F32)

        logits = lax.fori_loop(0, nv, body, jnp.zeros((rows, width), F32))
        top = jnp.max(logits, axis=1, keepdims=True)
        total = jnp.sum(jnp.exp(logits - top), axis=1, keepdims=True)
        yes = jnp.sum(jnp.where(cols == ids_ref[0:1, 0:1], logits, 0.0), axis=1, keepdims=True)
        no = jnp.sum(jnp.where(cols == ids_ref[1:2, 0:1], logits, 0.0), axis=1, keepdims=True)
        tile = jnp.where(lane == 0, top, 0.0)
        for at, what in ((1, total), (2, yes), (3, no)):
            tile = jnp.where(lane == at, what, tile)
        if tail is not None:
            tile = jnp.concatenate([tile, tail], axis=0)
        stat[e] = jnp.transpose(tile)[0:8]

    stats = []

    def deliver(e, at):
        copy = remote(
            stat.at[e], statr.at[me], t_send.at[at], t_recv.at[me], (e, col))
        copy.start()
        stats.append(copy)

    def finish(s):
        other = lines[s] + 1 - 2 * core
        for v in range(nv):
            arrived(other, v)
        head(other)
        deliver(other, 2 * s + 1)

    spread(0)
    for s in range(nz):
        if s + 1 < nz:
            spread(s + 1)
        collect(s)
        head(lines[s])
        if s:
            deliver(lines[s], 2 * s)
            finish(s - 1)
    finish(nz - 1)
    statr[me] = stat[me]
    for j in dpeer:
        e = dpeer[j]
        remote(
            stat.at[e], statr.at[e], t_send.at[0], t_recv.at[e], (e, col)
        ).wait_recv()

    def merge(ref, count):
        top = ref[0, 0:1]
        for e in range(1, count):
            top = jnp.maximum(top, ref[e, 0:1])
        total = jnp.zeros_like(top)
        yes = jnp.zeros_like(top)
        no = jnp.zeros_like(top)
        for e in range(count):
            total = total + ref[e, 1:2] * jnp.exp(ref[e, 0:1] - top)
            yes = yes + ref[e, 2:3]
            no = no + ref[e, 3:4]
        return top, total, yes, no

    top, total, yes, no = merge(statr, nd)
    vrow[col] = jnp.concatenate(
        [top, total, yes, no, jnp.zeros((4, top.shape[1]), F32)], axis=0)
    last = {}
    for j in vpeer:
        last[j] = remote(
            vrow.at[col], vrow.at[col], v_send.at[j], v_recv.at[col], (me, vpeer[j]))
        last[j].start()
    for j in vpeer:
        v = vpeer[j]
        remote(
            vrow.at[v], vrow.at[v], v_send.at[0], v_recv.at[v], (me, v)
        ).wait_recv()
    top, total, yes, no = merge(vrow, nv)
    log_total = top + jnp.log(total)
    out_ref[...] = jnp.concatenate(
        [yes - log_total, no - log_total, jnp.zeros((6, top.shape[1]), F32)], axis=0)
    for copy in [*parts.values(), *exch.values(), *sent, *stats, *last.values()]:
        copy.wait_send()


def dma(*shape):
    return pltpu.SemaphoreType.DMA(shape)


def selectors(pairs, answers, group, span, slots, each):
    prompts, per_prompt, _ = pairs.shape
    ids = jnp.arange(answers, dtype=jnp.int32)
    chosen = pairs[:, None, :, :] == ids[None, :, None, None]
    involved = chosen[..., 0] | chosen[..., 1]
    k = jnp.arange(per_prompt, dtype=jnp.int32)
    rank = jnp.sum(
        (involved[:, :, None, :] & (k[None, :] < k[:, None])[None, None]).astype(jnp.int32), -1)
    key = pairs * span + jnp.sum(
        jnp.where(chosen, rank[..., None], 0), axis=1) * group
    wide = jnp.repeat(key, group, axis=1) + jnp.tile(
        jnp.arange(group, dtype=jnp.int32), per_prompt)[None, :, None]
    wide = jnp.pad(wide, ((0, 0), (0, slots - wide.shape[1]), (0, 0)), constant_values=-1)
    row = jnp.arange(answers * span, dtype=jnp.int32)
    first, second = wide[:, :, 0], wide[:, :, 1]
    pick = (row[None, :, None] == first[:, None, :]) | (row[None, :, None] == second[:, None, :])
    both = jnp.pad(
        key, ((0, 0), (0, each - per_prompt), (0, 0)), constant_values=-group)
    both = both.transpose(0, 2, 1)[:, :, None, :] + jnp.arange(
        group, dtype=jnp.int32)[None, None, :, None]
    both = both.reshape(prompts, 2 * group * each)
    place = both[:, :, None] == row[None, None, :]
    return pick.astype(BF16), place.astype(BF16)


def local(
    queries, residual, cache_k, cache_v, lengths, pairs, out_weight, norm_gain,
    head_weight, answer_ids,
):
    nd, nv = lax.axis_size("dp"), lax.axis_size("vocab")
    answers, prompts, heads, longest, hd = cache_k.shape
    pair_rows = queries.shape[0]
    per_prompt = pairs.shape[1]
    group = queries.shape[1] // hd // heads
    span = up((answers - 1) * group, 16)
    slots = up(per_prompt * group, 16)
    each = up(per_prompt, 8)
    rows = prompts * each
    pick, place = selectors(pairs, answers, group, span, slots, each)
    q = queries.reshape(prompts, per_prompt, heads, group, hd).transpose(0, 2, 1, 3, 4)
    q = q.reshape(prompts, heads, per_prompt * group, hd)
    q = jnp.pad(q, ((0, 0), (0, 0), (0, slots - per_prompt * group), (0, 0)))
    lens = jnp.pad(lengths.T, ((0, 0), (0, up(prompts, 8) - prompts)))
    lens = jnp.broadcast_to(lens[:, :, None], lens.shape + (128,))
    vm = pl.BlockSpec(memory_space=pltpu.VMEM)
    hbm = pl.BlockSpec(memory_space=pl.ANY)
    attended = pl.pallas_call(
        functools.partial(attend_kernel, nd),
        out_shape=jax.ShapeDtypeStruct((rows, queries.shape[1]), BF16),
        in_specs=[vm, vm, vm, vm, hbm, hbm],
        out_specs=vm,
        scratch_shapes=[
            pltpu.VMEM(cache_k.shape, BF16),
            pltpu.VMEM(cache_k.shape, BF16),
            pltpu.VMEM((prompts, heads, answers * span, hd), BF16),
            pltpu.VMEM((answers, prompts, heads, span, hd), BF16),
            pltpu.VMEM(lens.shape, jnp.int32),
            pltpu.VMEM((answers, prompts, heads, span, hd), BF16),
            pltpu.VMEM((prompts, heads, answers * span, hd), BF16),
            pltpu.VMEM((answers, span, 128), BF16),
            pltpu.VMEM((answers * span, 128), BF16),
            dma(2, answers),
        ] + [dma(answers)] * 8,
        compiler_params=pltpu.CompilerParams(
            collective_id=0, has_side_effects=True, vmem_limit_bytes=56 << 20),
    )(pick, place, q, lens, cache_k, cache_v)
    share = residual.shape[1]
    width = head_weight.shape[1]
    res = jnp.pad(
        residual.reshape(prompts, per_prompt, share),
        ((0, 0), (0, each - per_prompt), (0, 0))).reshape(rows, share)
    chunk = min(share, 1024)
    own_gain = lax.dynamic_slice_in_dim(norm_gain, lax.axis_index("vocab") * share, share, 0)
    own_gain = jnp.broadcast_to(own_gain.astype(F32)[None], (8, share))
    ids = jnp.broadcast_to(jnp.pad(answer_ids, (0, 6))[:, None], (8, 128))
    wide = up(rows, 128)
    verdict = pl.pallas_call(
        functools.partial(tail_kernel, nd, nv, width, chunk),
        out_shape=jax.ShapeDtypeStruct((8, wide), F32),
        in_specs=[vm, hbm] + [vm] * 4,
        out_specs=vm,
        scratch_shapes=[
            pltpu.VMEM((BUFS, attended.shape[1], chunk), BF16),
            pltpu.VMEM((rows, share), F32),
            pltpu.VMEM((nv, rows, share), BF16),
            pltpu.VMEM((nv, rows, share), BF16),
            pltpu.VMEM((rows, share), BF16),
            pltpu.VMEM((rows, 128), F32),
            pltpu.VMEM((nv, rows, 128), F32),
            pltpu.VMEM((nd, nv, rows, share), BF16),
            pltpu.VMEM((nd, 8, wide), F32),
            pltpu.VMEM((nd, 8, wide), F32),
            pltpu.VMEM((nv, 8, wide), F32),
            dma(BUFS), dma(nv, share // chunk), dma(nv, share // chunk), dma(nv), dma(nv),
            dma((nd // 2) * (2 * nv + 1)), dma(nd, nv),
            dma(nd), dma(nd), dma(nv), dma(nv),
        ],
        compiler_params=pltpu.CompilerParams(
            collective_id=1, has_side_effects=True, vmem_limit_bytes=52 << 20),
    )(attended, out_weight, res, own_gain, head_weight.reshape(nv, share, width), ids)
    verdict = verdict[:2, :rows].reshape(2, prompts, each)[:, :, :per_prompt]
    return verdict.reshape(2, pair_rows).T


def solution(mesh):
    in_specs = (
        P("dp", "vocab"),
        P("dp", "vocab"),
        P(None, "dp", "vocab", None, None),
        P(None, "dp", "vocab", None, None),
        P("dp", None),
        P("dp", None, None),
        P("vocab", None),
        P(),
        P(None, ("dp", "vocab")),
        P(),
    )
    out_specs = P("dp", None)
    return jax.shard_map(local, mesh=mesh, in_specs=in_specs, out_specs=out_specs, check_vma=False)
```

```python
import functools
import math

import jax
import jax.numpy as jnp
from jax import lax
from jax.experimental import pallas as pl
from jax.experimental.pallas import tpu as pltpu
from jax.sharding import PartitionSpec as P

MESH = pl.DeviceIdType.MESH
F32 = jnp.float32
BF16 = jnp.bfloat16
BUFS = 4


def up(n, m):
    return -(-n // m) * m


def remote(src, dst, send, recv, device):
    return pltpu.make_async_remote_copy(
        src_ref=src, dst_ref=dst, send_sem=send, recv_sem=recv,
        device_id=device, device_id_type=MESH,
    )


def greet(partners):
    barrier = pltpu.get_barrier_semaphore()
    for device in partners:
        pl.semaphore_signal(barrier, inc=1, device_id=device, device_id_type=MESH)
    pl.semaphore_wait(barrier, len(partners))


def attend_kernel(
    n, pick_ref, place_ref, q_ref, lens_ref, k_hbm, v_hbm, out_ref,
    k_ref, v_ref, qs, qr, lr, ob, orecv, st, strecv,
    kv_sem, q_send, q_recv, l_send, l_recv, o_send, o_recv, s_send, s_recv,
):
    answers, prompts, heads, longest, hd = k_hbm.shape
    span = qr.shape[3]
    me, col = lax.axis_index("dp"), lax.axis_index("vocab")
    loads = []
    for i in range(answers):
        for which, (src, dst) in enumerate(((k_hbm, k_ref), (v_hbm, v_ref))):
            load = pltpu.make_async_copy(src.at[i], dst.at[i], kv_sem.at[which, i])
            load.start()
            loads.append(load)
    shifts = sorted({s % n for i in range(1, answers) for s in (i, -i)})
    for p in range(prompts):
        for c in range(heads):
            qs[p, c] = jnp.dot(
                pick_ref[p], q_ref[p, c], preferred_element_type=F32
            ).astype(BF16)
    greet([(lax.rem(me + s, n), col) for s in shifts])
    order = [1, 2, 6, 3, 5, 4] if answers == 7 else list(range(1, answers))
    q_out, l_out, o_out, s_out = {}, {}, {}, {}
    for i in order:
        ahead = (lax.rem(me + i, n), col)
        behind = (lax.rem(me + n - i, n), col)
        rows = pl.ds(i * span, span)
        q_out[i] = remote(
            qs.at[:, :, rows], qr.at[i], q_send.at[i], q_recv.at[i], ahead)
        l_out[i] = remote(lens_ref.at[i], lr.at[i], l_send.at[i], l_recv.at[i], ahead)
        o_out[i] = remote(
            ob.at[i], orecv.at[:, :, rows], o_send.at[i], o_recv.at[i], behind)
        s_out[i] = remote(
            st.at[i], strecv.at[rows], s_send.at[i], s_recv.at[i], behind)
        q_out[i].start()
        l_out[i].start()
    scale = 1.0 / math.sqrt(hd)
    for i in [0] + order:
        loads[2 * i].wait()
        loads[2 * i + 1].wait()
        if i:
            q_out[i].wait_recv()
            l_out[i].wait_recv()
        lane = lax.broadcasted_iota(jnp.int32, (span, 128), 1)
        position = lax.broadcasted_iota(jnp.int32, (span, longest), 1)
        stats = jnp.zeros((span, 128), F32)
        for p in range(prompts):
            limit = (lr[i, p : p + 1, 0:1] if i else lens_ref[0, p : p + 1, 0:1])
            for c in range(heads):
                q = qr[i, p, c] if i else qs[p, c, 0:span]
                s = lax.dot_general(
                    q, k_ref[i, p, c], (((1,), (1,)), ((), ())),
                    preferred_element_type=F32,
                ) * scale
                s = jnp.where(position < limit, s, -jnp.inf)
                top = jnp.max(s, axis=1, keepdims=True)
                e = jnp.exp(s - top)
                total = jnp.sum(e, axis=1, keepdims=True)
                big = e.astype(BF16)
                small = (e - big.astype(F32)).astype(BF16)
                o = jnp.dot(big, v_ref[i, p, c], preferred_element_type=F32)
                o = o + jnp.dot(small, v_ref[i, p, c], preferred_element_type=F32)
                o = (o / total).astype(BF16)
                if i:
                    ob[i, p, c] = o
                else:
                    orecv[p, c, 0:span] = o
                lse = top + jnp.log(total)
                high = lse.astype(BF16).astype(F32)
                mid = (lse - high).astype(BF16).astype(F32)
                low = lse - high - mid
                at = 3 * (p * heads + c)
                stats = jnp.where(lane == at, high, stats)
                stats = jnp.where(lane == at + 1, mid, stats)
                stats = jnp.where(lane == at + 2, low, stats)
        if i:
            st[i] = stats.astype(BF16)
            o_out[i].start()
            s_out[i].start()
        else:
            strecv[0:span] = stats.astype(BF16)
    for i in order:
        o_out[i].wait_recv()
        s_out[i].wait_recv()
    half = place_ref.shape[1] // 2
    group = out_ref.shape[1] // heads // hd
    each = half // group
    for p in range(prompts):
        place = place_ref[p]
        both = jnp.dot(place, strecv[...], preferred_element_type=F32)
        for c in range(heads):
            at = 3 * (p * heads + c)
            lse = both[:, at : at + 1] + both[:, at + 1 : at + 2] + both[:, at + 2 : at + 3]
            first, second = lse[:half], lse[half:]
            top = jnp.maximum(first, second)
            first, second = jnp.exp(first - top), jnp.exp(second - top)
            o = jnp.dot(place, orecv[p, c], preferred_element_type=F32)
            mixed = (first * o[:half] + second * o[half:]) / (first + second)
            mixed = mixed.astype(BF16)
            for j in range(group):
                at = (c * group + j) * hd
                out_ref[p * each : (p + 1) * each, at : at + hd] = (
                    mixed[j * each : (j + 1) * each])
    for i in order:
        for copy in (q_out[i], l_out[i], o_out[i], s_out[i]):
            copy.wait_send()


def tail_kernel(
    nd, nv, width, chunk, att_ref, ow_hbm, res_ref, gain_ref, w_ref, ids_ref, out_ref,
    wb, own, sb, rb, hid, sq, sqr, g, stat, statr, vrow,
    w_sem, p_send, p_recv, q_send, q_recv, g_send, g_recv, t_send, t_recv, v_send, v_recv,
):
    rows, share = res_ref.shape
    me, col = lax.axis_index("dp"), lax.axis_index("vocab")
    square = nv == 4
    if square:
        vpeer = {
            3: 3 - col, 1: col + 1 - 2 * lax.rem(col, 2), 2: lax.rem(col + 2, nv)}
    else:
        vpeer = {j: lax.rem(col + j, nv) for j in range(1, nv)}
    dpeer = {j: lax.rem(me + j, nd) for j in range(1, nd)}
    per = share // chunk
    todo = [(j, t) for j in [*vpeer, 0] for t in range(per)]

    def load(at):
        j, t = todo[at]
        v = vpeer[j] if j else col
        start = pl.multiple_of(v * share + t * chunk, 128)
        return pltpu.make_async_copy(
            ow_hbm.at[:, pl.ds(start, chunk)], wb.at[at % BUFS], w_sem.at[at % BUFS])

    for at in range(min(BUFS, len(todo))):
        load(at).start()
    greet([(me, vpeer[j]) for j in vpeer] + [(dpeer[j], col) for j in dpeer])
    step = 256 if chunk % 256 == 0 else 128
    parts = {}
    for at, (j, t) in enumerate(todo):
        load(at).wait()

        def tile(u, carry, at=at, j=j, t=t):
            here = pl.ds(pl.multiple_of(u * step, step), step)
            there = pl.ds(pl.multiple_of(t * chunk + u * step, step), step)
            got = jnp.dot(
                att_ref[...], wb[at % BUFS, :, here], preferred_element_type=F32)
            if j:
                sb[j, :, there] = got.astype(BF16)
            else:
                own[:, there] = got + res_ref[:, there].astype(F32)
            return carry

        lax.fori_loop(0, chunk // step, tile, 0)
        if at + BUFS < len(todo):
            load(at + BUFS).start()
        if j:
            there = pl.ds(t * chunk, chunk)
            parts[j, t] = remote(
                sb.at[j, :, there], rb.at[j, :, there],
                p_send.at[j, t], p_recv.at[j, t], (me, vpeer[j]))
            parts[j, t].start()
    squares = jnp.zeros((rows, 128), F32)
    for t in range(0, share, step):
        if t % chunk == 0:
            for j in vpeer:
                parts[j, t // chunk].wait_recv()
        total = own[:, t : t + step]
        for j in vpeer:
            total = total + rb[j, :, t : t + step].astype(F32)
        total = total.astype(BF16)
        hid[:, t : t + step] = total
        total = total.astype(F32)
        for u in range(0, step, 128):
            squares = squares + total[:, u : u + 128] * total[:, u : u + 128]
    sq[...] = squares
    exch = {}
    for j in vpeer:
        exch[j] = remote(
            sq, sqr.at[j], q_send.at[j], q_recv.at[j], (me, vpeer[j]))
        exch[j].start()
    for j in vpeer:
        exch[j].wait_recv()
        squares = squares + sqr[j]
    mean = jnp.sum(squares, axis=1, keepdims=True) * (1.0 / (share * nv))
    factor = lax.rsqrt(mean + 1e-05)
    for t in range(0, share, step):
        block = hid[:, t : t + step].astype(F32) * factor
        g[me, col, :, t : t + step] = (
            block * gain_ref[0:1, t : t + step].astype(F32)
        ).astype(BF16)

    core = lax.rem(me, 2)
    sib = me + 1 - 2 * core
    sent = []

    def push(e, v, device, slot):
        block = g.at[e, v]
        copy = remote(block, block, g_send.at[slot], g_recv.at[e, v], device)
        copy.start()
        sent.append(copy)

    def arrived(e, v):
        block = g.at[e, v]
        remote(block, block, g_send.at[0], g_recv.at[e, v], (sib, col)).wait_recv()

    nz = nd // 2
    z = lax.div(me, 2)
    upper = lax.div(z, nz // 2)
    mirrored = z + upper * (nz - 1 - 2 * z)
    lines = [me]
    for t in range(nz - 1):
        at = t + lax.div(t - mirrored + nz, nz)
        lines.append(2 * (at + upper * (nz - 1 - 2 * at)) + core)
    slot = [0]

    def send(e, v, device):
        push(e, v, device, slot[0])
        slot[0] += 1

    direct = [1, 2] if square else list(vpeer)

    def spread(s):
        e = lines[s]
        if s:
            arrived(e, col)
        for j in direct:
            send(e, col, (me, vpeer[j]))
        if s == 0:
            for t in reversed(range(1, nz)):
                send(e, col, (lines[t], col))
        send(e, col, (sib, col))

    def collect(s):
        e = lines[s]
        for j in direct:
            arrived(e, vpeer[j])
            if square and j == 1 + s % 2:
                send(e, vpeer[j], (me, vpeer[3 - j]))
            send(e, vpeer[j], (sib, col))
        if square:
            arrived(e, vpeer[3])
            send(e, vpeer[3], (sib, col))

    base = (me * nv + col) * width
    cols = lax.broadcasted_iota(jnp.int32, (rows, width), 1) + base
    lane = lax.broadcasted_iota(jnp.int32, (rows, 128), 1)
    tail = jnp.zeros((128 - rows % 128, 128), F32) if rows % 128 else None

    def head(start):
        def body(v, acc):
            block = g[pl.ds(start, 2), v].reshape(2 * rows, share)
            return acc + jnp.dot(block, w_ref[v], preferred_element_type=F32)

        both = lax.fori_loop(0, nv, body, jnp.zeros((2 * rows, width), F32))
        for half in range(2):
            logits = both[half * rows : (half + 1) * rows]
            top = jnp.max(logits, axis=1, keepdims=True)
            total = jnp.sum(jnp.exp(logits - top), axis=1, keepdims=True)
            yes = jnp.sum(
                jnp.where(cols == ids_ref[0:1, 0:1], logits, 0.0), axis=1, keepdims=True)
            no = jnp.sum(
                jnp.where(cols == ids_ref[1:2, 0:1], logits, 0.0), axis=1, keepdims=True)
            tile = jnp.where(lane == 0, top, 0.0)
            for at, what in ((1, total), (2, yes), (3, no)):
                tile = jnp.where(lane == at, what, tile)
            if tail is not None:
                tile = jnp.concatenate([tile, tail], axis=0)
            stat[start + half] = jnp.transpose(tile)[0:8]

    stats = []

    def deliver(e, at):
        copy = remote(
            stat.at[e], statr.at[me], t_send.at[at], t_recv.at[me], (e, col))
        copy.start()
        stats.append(copy)

    def finish(s):
        other = lines[s] + 1 - 2 * core
        for v in range(nv):
            arrived(other, v)
        head(lines[s] - core)
        if s:
            deliver(lines[s], 2 * s)
        deliver(other, 2 * s + 1)

    spread(0)
    for s in range(nz):
        if s + 1 < nz:
            spread(s + 1)
        collect(s)
        if s:
            finish(s - 1)
    finish(nz - 1)
    statr[me] = stat[me]
    for j in dpeer:
        e = dpeer[j]
        remote(
            stat.at[e], statr.at[e], t_send.at[0], t_recv.at[e], (e, col)
        ).wait_recv()

    def merge(ref, count):
        top = ref[0, 0:1]
        for e in range(1, count):
            top = jnp.maximum(top, ref[e, 0:1])
        total = jnp.zeros_like(top)
        yes = jnp.zeros_like(top)
        no = jnp.zeros_like(top)
        for e in range(count):
            total = total + ref[e, 1:2] * jnp.exp(ref[e, 0:1] - top)
            yes = yes + ref[e, 2:3]
            no = no + ref[e, 3:4]
        return top, total, yes, no

    top, total, yes, no = merge(statr, nd)
    vrow[col] = jnp.concatenate(
        [top, total, yes, no, jnp.zeros((4, top.shape[1]), F32)], axis=0)
    last = {}
    for j in vpeer:
        last[j] = remote(
            vrow.at[col], vrow.at[col], v_send.at[j], v_recv.at[col], (me, vpeer[j]))
        last[j].start()
    for j in vpeer:
        v = vpeer[j]
        remote(
            vrow.at[v], vrow.at[v], v_send.at[0], v_recv.at[v], (me, v)
        ).wait_recv()
    top, total, yes, no = merge(vrow, nv)
    log_total = top + jnp.log(total)
    out_ref[...] = jnp.concatenate(
        [yes - log_total, no - log_total, jnp.zeros((6, top.shape[1]), F32)], axis=0)
    for copy in [*parts.values(), *exch.values(), *sent, *stats, *last.values()]:
        copy.wait_send()


def dma(*shape):
    return pltpu.SemaphoreType.DMA(shape)


def selectors(pairs, answers, group, span, slots, each):
    prompts, per_prompt, _ = pairs.shape
    ids = jnp.arange(answers, dtype=jnp.int32)
    chosen = pairs[:, None, :, :] == ids[None, :, None, None]
    involved = chosen[..., 0] | chosen[..., 1]
    k = jnp.arange(per_prompt, dtype=jnp.int32)
    rank = jnp.sum(
        (involved[:, :, None, :] & (k[None, :] < k[:, None])[None, None]).astype(jnp.int32), -1)
    key = pairs * span + jnp.sum(
        jnp.where(chosen, rank[..., None], 0), axis=1) * group
    wide = jnp.repeat(key, group, axis=1) + jnp.tile(
        jnp.arange(group, dtype=jnp.int32), per_prompt)[None, :, None]
    wide = jnp.pad(wide, ((0, 0), (0, slots - wide.shape[1]), (0, 0)), constant_values=-1)
    row = jnp.arange(answers * span, dtype=jnp.int32)
    first, second = wide[:, :, 0], wide[:, :, 1]
    pick = (row[None, :, None] == first[:, None, :]) | (row[None, :, None] == second[:, None, :])
    both = jnp.pad(
        key, ((0, 0), (0, each - per_prompt), (0, 0)), constant_values=-group)
    both = both.transpose(0, 2, 1)[:, :, None, :] + jnp.arange(
        group, dtype=jnp.int32)[None, None, :, None]
    both = both.reshape(prompts, 2 * group * each)
    place = both[:, :, None] == row[None, None, :]
    return pick.astype(BF16), place.astype(BF16)


def local(
    queries, residual, cache_k, cache_v, lengths, pairs, out_weight, norm_gain,
    head_weight, answer_ids,
):
    nd, nv = lax.axis_size("dp"), lax.axis_size("vocab")
    answers, prompts, heads, longest, hd = cache_k.shape
    pair_rows = queries.shape[0]
    per_prompt = pairs.shape[1]
    group = queries.shape[1] // hd // heads
    span = up((answers - 1) * group, 16)
    slots = up(per_prompt * group, 16)
    each = up(per_prompt, 8)
    rows = prompts * each
    pick, place = selectors(pairs, answers, group, span, slots, each)
    q = queries.reshape(prompts, per_prompt, heads, group, hd).transpose(0, 2, 1, 3, 4)
    q = q.reshape(prompts, heads, per_prompt * group, hd)
    q = jnp.pad(q, ((0, 0), (0, 0), (0, slots - per_prompt * group), (0, 0)))
    lens = jnp.pad(lengths.T, ((0, 0), (0, up(prompts, 8) - prompts)))
    lens = jnp.broadcast_to(lens[:, :, None], lens.shape + (128,))
    vm = pl.BlockSpec(memory_space=pltpu.VMEM)
    hbm = pl.BlockSpec(memory_space=pl.ANY)
    attended = pl.pallas_call(
        functools.partial(attend_kernel, nd),
        out_shape=jax.ShapeDtypeStruct((rows, queries.shape[1]), BF16),
        in_specs=[vm, vm, vm, vm, hbm, hbm],
        out_specs=vm,
        scratch_shapes=[
            pltpu.VMEM(cache_k.shape, BF16),
            pltpu.VMEM(cache_k.shape, BF16),
            pltpu.VMEM((prompts, heads, answers * span, hd), BF16),
            pltpu.VMEM((answers, prompts, heads, span, hd), BF16),
            pltpu.VMEM(lens.shape, jnp.int32),
            pltpu.VMEM((answers, prompts, heads, span, hd), BF16),
            pltpu.VMEM((prompts, heads, answers * span, hd), BF16),
            pltpu.VMEM((answers, span, 128), BF16),
            pltpu.VMEM((answers * span, 128), BF16),
            dma(2, answers),
        ] + [dma(answers)] * 8,
        compiler_params=pltpu.CompilerParams(
            collective_id=0, has_side_effects=True, vmem_limit_bytes=56 << 20),
    )(pick, place, q, lens, cache_k, cache_v)
    share = residual.shape[1]
    width = head_weight.shape[1]
    res = jnp.pad(
        residual.reshape(prompts, per_prompt, share),
        ((0, 0), (0, each - per_prompt), (0, 0))).reshape(rows, share)
    chunk = min(share, 1024)
    own_gain = lax.dynamic_slice_in_dim(norm_gain, lax.axis_index("vocab") * share, share, 0)
    own_gain = jnp.broadcast_to(own_gain.astype(F32)[None], (8, share))
    ids = jnp.broadcast_to(jnp.pad(answer_ids, (0, 6))[:, None], (8, 128))
    wide = up(rows, 128)
    verdict = pl.pallas_call(
        functools.partial(tail_kernel, nd, nv, width, chunk),
        out_shape=jax.ShapeDtypeStruct((8, wide), F32),
        in_specs=[vm, hbm] + [vm] * 4,
        out_specs=vm,
        scratch_shapes=[
            pltpu.VMEM((BUFS, attended.shape[1], chunk), BF16),
            pltpu.VMEM((rows, share), F32),
            pltpu.VMEM((nv, rows, share), BF16),
            pltpu.VMEM((nv, rows, share), BF16),
            pltpu.VMEM((rows, share), BF16),
            pltpu.VMEM((rows, 128), F32),
            pltpu.VMEM((nv, rows, 128), F32),
            pltpu.VMEM((nd, nv, rows, share), BF16),
            pltpu.VMEM((nd, 8, wide), F32),
            pltpu.VMEM((nd, 8, wide), F32),
            pltpu.VMEM((nv, 8, wide), F32),
            dma(BUFS), dma(nv, share // chunk), dma(nv, share // chunk), dma(nv), dma(nv),
            dma((nd // 2) * (2 * nv + 1)), dma(nd, nv),
            dma(nd), dma(nd), dma(nv), dma(nv),
        ],
        compiler_params=pltpu.CompilerParams(
            collective_id=1, has_side_effects=True, vmem_limit_bytes=52 << 20),
    )(attended, out_weight, res, own_gain, head_weight.reshape(nv, share, width), ids)
    verdict = verdict[:2, :rows].reshape(2, prompts, each)[:, :, :per_prompt]
    return verdict.reshape(2, pair_rows).T


def solution(mesh):
    in_specs = (
        P("dp", "vocab"),
        P("dp", "vocab"),
        P(None, "dp", "vocab", None, None),
        P(None, "dp", "vocab", None, None),
        P("dp", None),
        P("dp", None, None),
        P("vocab", None),
        P(),
        P(None, ("dp", "vocab")),
        P(),
    )
    out_specs = P("dp", None)
    return jax.shard_map(local, mesh=mesh, in_specs=in_specs, out_specs=out_specs, check_vma=False)
```
